512 devices in a mesh: row: 32 (over y, x), col: 16 (over z, core).
Axes of the slice: x: 4, y: 8, z: 8, core: 2. Of those that a mesh axis runs over, the one named last changes fastest.
Arguments:
- tiles: float32 [32, 16, 2, 256, 256], P('row', 'col'), may hold values from -0.375 to 0.375
- tile_rows: int32 [32, 16, 2], P('row', 'col'), may hold values from 0 to 7
- tile_cols: int32 [32, 16, 2], P('row', 'col'), may hold values from 0 to 15, as said below
- tile_counts: int32 [32, 16], P('row', 'col'), may hold values from 1 to 2, as said below
- diagonal: float32 [65536], P(('row', 'col')), may hold values from 0.5 to 4
- basis: float32 [16, 16, 65536], P(None, None, ('row', 'col')), may hold values from -6 to 6
- start: float32 [16, 65536], P(None, ('row', 'col')), may hold values from -8 to 8
Outputs:
- blocks: float32 [2, 16, 65536], P(None, None, ('row', 'col'))
- factors: float32 [2, 16, 16], replicated
The draws below stay inside these ranges and needn't reach their ends.
Inputs may be any that keep to these rules, and one draw needn't show every extreme that they name: `tile_cols`: the slots of one device name distinct tile-column blocks. `tile_counts`: slots from this count on are padding.
All inputs are finite; a program needn't handle non-finite values.
Results may differ from the reference program's by a relative error of at most 0.004.
Values may be sent and summed in bfloat16 or wider, within the bound.
A program may use at most 64 MiB of HBM per device.

```python
import math
import jax
import jax.numpy as jnp
from jax import lax

TILE = 256
BW = 16
BLK_ROW = 8
TILES_DEV = 2
NBAS = 16
RGRP = 32
CGRP = 16
N = 65536


def tile_pattern(key):
    devices = RGRP * CGRP
    key_cols, key_rows, key_one, key_two, key_busy = jax.random.split(key, 5)
    col_keys = jax.random.split(key_cols, devices)
    spread = 2 * BLK_ROW
    picked = jax.vmap(lambda each: jax.random.permutation(each, spread)[:TILES_DEV])(col_keys).astype(jnp.int32)
    rows = jax.random.randint(key_rows, (devices, TILES_DEV), 0, BLK_ROW).astype(jnp.int32)
    first_pick = jax.random.randint(key_one, (devices,), 0, TILES_DEV)
    second_pick = jax.random.randint(key_two, (devices,), 0, TILES_DEV)
    counts = 1 + first_pick * second_pick // (TILES_DEV - 1)
    busiest = jax.random.randint(key_busy, (), 0, devices)
    slot_index = jnp.arange(TILES_DEV)
    chosen = jnp.arange(devices) == busiest
    busy_cols = jnp.where(slot_index == 1, 0, spread - 1 - slot_index)
    busy_rows = jnp.where(slot_index == 0, BLK_ROW - 1, jnp.where(slot_index == 1, 0, rows[busiest]))
    cols = jnp.where(chosen[:, None], busy_cols[None, :], picked)
    rows = jnp.where(chosen[:, None], busy_rows[None, :], rows)
    counts = jnp.where(chosen, TILES_DEV, counts)
    return (rows.reshape(RGRP, CGRP, TILES_DEV).astype(jnp.int32), cols.reshape(RGRP, CGRP, TILES_DEV).astype(jnp.int32), counts.reshape(RGRP, CGRP).astype(jnp.int32))


def basis_normal(key):
    values = jax.random.normal(jax.random.fold_in(key, 77), (NBAS, BW, N), jnp.float32)
    return jnp.clip(values, -6.0, 6.0)


def draw_tile_rows(key, part):
    shared = tile_pattern(key)
    return shared[0]


def draw_tile_cols(key, part):
    shared = tile_pattern(key)
    return shared[1]


def draw_tile_counts(key, part):
    shared = tile_pattern(key)
    return shared[2]


def draw_basis(key, part):
    shared = basis_normal(key)
    return shared


def draw_start(key, part):
    shared = basis_normal(key)
    key = jax.random.fold_in(key, 9)
    own_part = jax.random.normal(key, (BW, N), jnp.float32)
    return jnp.clip(own_part + 0.3 * jnp.sum(shared, axis=0), -8.0, 8.0)


def level_of(own_key, dims, cuts, smallest, high):
    gain, own = 1.0, jax.random.fold_in(own_key, 6)
    for axis_at, parts in cuts:
        steps = jnp.exp(jax.random.uniform(jax.random.fold_in(own, axis_at), (parts,), jnp.float32, smallest / len(cuts), high / len(cuts)))
        gain = gain * jnp.repeat(steps, dims[axis_at] // parts).reshape([-1 if axis == axis_at else 1 for axis in range(len(dims))])
    return gain


def bell_draw(key, shape, scale, limit, cuts=(), kind=jnp.bfloat16):
    level = level_of(key, shape, cuts, -0.22, 0.18) if cuts else 1.0
    entries = jax.random.normal(key, shape, jnp.float32) * scale * level
    return jnp.minimum(jnp.maximum(entries, -limit), limit).astype(kind)


def setup_inputs(seed: int = 0) -> dict:
    keys = jax.random.split(jax.random.key(seed), 8)
    return {
        "tiles": bell_draw(keys[0], (RGRP, CGRP, TILES_DEV, TILE, TILE), TILE ** -0.5, 0.375, ((0, 32), (1, 16)), jnp.float32),
        "tile_rows": draw_tile_rows(jax.random.fold_in(keys[7], 71), 0),
        "tile_cols": draw_tile_cols(jax.random.fold_in(keys[7], 71), 0),
        "tile_counts": draw_tile_counts(jax.random.fold_in(keys[7], 71), 0),
        "diagonal": jnp.clip(jnp.exp(math.log(4.0) - 2.0794415 * jax.random.uniform(keys[4], (N,), jnp.float32) ** level_of(keys[4], (N,), ((0, 512),), -0.2, 0.2)), 0.5, 4.0),
        "basis": draw_basis(jax.random.fold_in(keys[7], 71), 0),
        "start": draw_start(jax.random.fold_in(keys[7], 71), 0),
    }


PRECISE = lax.Precision.HIGHEST

def apply_tiles(field, tiles, tile_rows, tile_cols, tile_counts):
    row_count, col_count, slot_count = tile_rows.shape
    vec_width, total_rows = field.shape
    all_blocks = total_rows // TILE
    blocked = field.reshape(vec_width, all_blocks, TILE)
    flat_tiles = tiles.reshape(row_count * col_count, slot_count, TILE, TILE)
    flat_rows = tile_rows.reshape(row_count * col_count, slot_count)
    flat_cols = tile_cols.reshape(row_count * col_count, slot_count)
    flat_counts = tile_counts.reshape(row_count * col_count)
    places = jnp.arange(row_count * col_count, dtype=jnp.int32)
    zero_index = jnp.zeros((), jnp.int32)

    def visit(accum, item):
        plates, rows, cols, filled, place = item
        row_index = (place // col_count).astype(jnp.int32)
        col_index = (place % col_count).astype(jnp.int32)
        row_block = row_index * BLK_ROW + rows
        col_block = (col_index + col_count * (cols // BLK_ROW)) * BLK_ROW + cols % BLK_ROW
        is_live = jnp.arange(slot_count, dtype=jnp.int32) < filled
        factor = jnp.where(is_live, jnp.where(row_block == col_block, 0.5, 1.0), 0.0).astype(jnp.float32)
        from_cols = blocked[:, col_block, :]
        from_rows = blocked[:, row_block, :]
        row_terms = jnp.einsum('ksj,sij->ksi', from_cols, plates, precision=PRECISE) * factor[None, :, None]
        col_terms = jnp.einsum('ksi,sij->ksj', from_rows, plates, precision=PRECISE) * factor[None, :, None]
        row_pick = (rows[:, None] == jnp.arange(BLK_ROW, dtype=jnp.int32)[None, :]).astype(jnp.float32)
        col_pick = (cols[:, None] == jnp.arange(2 * BLK_ROW, dtype=jnp.int32)[None, :]).astype(jnp.float32)
        row_part = jnp.einsum('ksi,sa->kai', row_terms, row_pick, precision=PRECISE).astype(jnp.bfloat16)
        col_part = jnp.einsum('ksj,sb->kbj', col_terms, col_pick, precision=PRECISE).astype(jnp.bfloat16)
        row_part = lax.optimization_barrier(row_part).astype(jnp.float32)
        col_part = lax.optimization_barrier(col_part).astype(jnp.float32)
        row_start = (row_index * BLK_ROW).astype(jnp.int32)
        current = lax.dynamic_slice(accum, (zero_index, row_start, zero_index), (vec_width, BLK_ROW, TILE))
        accum = lax.dynamic_update_slice(accum, current + row_part, (zero_index, row_start, zero_index))
        for half_index in range(2):
            col_start = ((col_index + half_index * col_count) * BLK_ROW).astype(jnp.int32)
            current = lax.dynamic_slice(accum, (zero_index, col_start, zero_index), (vec_width, BLK_ROW, TILE))
            piece = col_part[:, half_index * BLK_ROW:(half_index + 1) * BLK_ROW, :]
            accum = lax.dynamic_update_slice(accum, current + piece, (zero_index, col_start, zero_index))
        return (accum, None)
    start_accum = jnp.zeros((vec_width, all_blocks, TILE), jnp.float32)
    accum, _ = lax.scan(visit, start_accum, (flat_tiles, flat_rows, flat_cols, flat_counts, places))
    return accum.reshape(vec_width, total_rows)

def reference(tiles, tile_rows, tile_cols, tile_counts, diagonal, basis, start):
    total_rows = start.shape[1]
    inv_total = 1.0 / total_rows
    stack_all = jnp.concatenate([basis, start[None]], axis=0)
    current = start
    outputs = []
    lowers = []
    for step_index in range(2):
        image_block = apply_tiles(current, tiles, tile_rows, tile_cols, tile_counts) + diagonal[None, :] * current
        first_proj = jnp.einsum('mkn,ln->mkl', stack_all, image_block, precision=PRECISE) * inv_total
        once_done = image_block - jnp.einsum('mkl,mkn->ln', first_proj, stack_all, precision=PRECISE)
        second_proj = jnp.einsum('mkn,ln->mkl', stack_all, once_done, precision=PRECISE) * inv_total
        twice_done = once_done - jnp.einsum('mkl,mkn->ln', second_proj, stack_all, precision=PRECISE)
        gram_block = jnp.dot(twice_done, twice_done.T, precision=PRECISE) * inv_total
        lower_factor = jnp.linalg.cholesky(gram_block)
        fresh_block = lax.linalg.triangular_solve(lower_factor, twice_done, left_side=True, lower=True)
        outputs.append(fresh_block)
        lowers.append(lower_factor)
        stack_all = jnp.concatenate([stack_all, fresh_block[None]], axis=0)
        current = fresh_block
    return (jnp.stack(outputs), jnp.stack(lowers))
```

```python
import functools

import jax
import jax.numpy as jnp
from jax import lax
from jax.experimental import pallas as pl
from jax.experimental.pallas import tpu as pltpu
from jax.sharding import PartitionSpec as P

MESH = pl.DeviceIdType.MESH
F32, BF16 = jnp.float32, jnp.bfloat16
HIGH = lax.Precision.HIGHEST
ROWS, COLS, YS, XS = 32, 16, 8, 4
BW, LANES, TILE = 16, 128, 256
KNOWN, FRESH, IMAGE, DEPTH = 272, 272, 288, 384


def dot(a, b, precision=HIGH):
    return lax.dot_general(a, b, (((1,), (0,)), ((), ())), precision=precision, preferred_element_type=F32)


def dot_t(a, b, precision=HIGH):
    return lax.dot_general(a, b, (((1,), (1,)), ((), ())), precision=precision, preferred_element_type=F32)


def at(row, col):
    return {"row": row, "col": col}


def push(src, dst, send_sem, recv_sem, target):
    pltpu.make_async_remote_copy(
        src_ref=src, dst_ref=dst, send_sem=send_sem, recv_sem=recv_sem, device_id=target, device_id_type=MESH
    ).start()


def drain(ref, sem):
    pltpu.make_async_copy(ref, ref, sem).wait()


def loop(low, high, body):
    def run(k, carry):
        body(k)
        return carry

    lax.fori_loop(low, high, run, 0)


def factor(gram):
    row = lax.broadcasted_iota(jnp.int32, (BW, LANES), 0)
    lane = lax.broadcasted_iota(jnp.int32, (BW, LANES), 1)
    eye = (lane == row + BW).astype(F32)
    work = jnp.concatenate([gram, jnp.zeros((BW, LANES - BW), F32)], axis=1) + eye
    lower = jnp.zeros((BW, LANES), F32)
    scale = jnp.zeros((BW, LANES), F32)
    for j in range(BW):
        pivot_row = work[j : j + 1, :]
        column = work[:, j : j + 1]
        pivot = pivot_row[:, j : j + 1]
        root = 1.0 / jnp.sqrt(pivot)
        lower = jnp.where((lane == j) & (row >= j), column * root, lower)
        scale = jnp.where(row == j, root, scale)
        step = jnp.where(row > j, column * (1.0 / pivot), 0.0)
        work = work - step * pivot_row
    inverse = (work * scale)[:, BW : 2 * BW]
    return lower[:, :BW], inverse


def kernel(
    tiles_ref, rows_ref, cols_ref, count_ref, diag_ref, basis_ref, start_ref,
    blocks_ref, factors_ref,
    stack, plates, split, dg, sent, vrow, vcol, prow, pcol, grow, gcol,
    c_part, c_col, c_sum, c_row, c_all, c_got,
    m_part, m_col, m_y, m_x, m_one, m_two, m_all, m_got, gram, clean,
    load_sem, v_send, vrow_sem, vcol_sem, p_send, grow_sem, gcol_sem, ar_send, ar_sem, m_send, m_sem,
):
    r, c = lax.axis_index("row"), lax.axis_index("col")
    y, x = r // XS, lax.rem(r, XS)
    twin = lax.rem(r, COLS)
    own = c == twin
    inv_total = 1.0 / (ROWS * COLS * LANES)

    loads = [
        pltpu.make_async_copy(basis_ref, stack.at[pl.ds(0, 256)], load_sem.at[0]),
        pltpu.make_async_copy(start_ref, stack.at[pl.ds(256, BW)], load_sem.at[1]),
        pltpu.make_async_copy(tiles_ref, plates, load_sem.at[2]),
        pltpu.make_async_copy(diag_ref, dg, load_sem.at[3]),
    ]
    for each in loads:
        each.start()

    barrier = pltpu.get_barrier_semaphore()

    def greet(target):
        pl.semaphore_signal(barrier, inc=1, device_id=target, device_id_type=MESH)

    def greet_rows(k):
        greet(at(lax.rem(r + k, ROWS), c))

    def greet_cols(k):
        greet(at(r, lax.rem(c + k, COLS)))

    def greet_twins(k):
        greet(at(lax.rem(r + k, ROWS), twin))
        greet(at(c + COLS * (k // COLS), lax.rem(k, COLS)))

    loop(0, ROWS, greet_twins)
    loop(1, ROWS, greet_rows)
    loop(1, COLS, greet_cols)

    stack[FRESH:DEPTH, :] = jnp.zeros((DEPTH - FRESH, LANES), F32)
    loads[0].wait()
    loads[1].wait()
    low, mid, last = stack[0:128, :], stack[128:256, :], stack[256:DEPTH, :][:BW]
    sent[0] = last.astype(BF16)
    m_part[:, 0] = dot_t(low, low).reshape(COLS, 8, LANES)
    m_part[:, 1] = dot_t(low, mid).reshape(COLS, 8, LANES)
    m_part[:, 2] = dot_t(mid, mid).reshape(COLS, 8, LANES)
    edge = dot_t(last, stack[...])
    m_part[:, 3] = jnp.zeros((COLS, 8, LANES), F32)
    for k in range(COLS):
        for j in range(3):
            m_part[k, 3, j : j + 1, :] = edge[k : k + 1, LANES * j : LANES * (j + 1)]
    m_col[c] = m_part[c]
    loads[2].wait()
    loads[3].wait()
    for s in range(2):
        whole = plates[s]
        high = whole.astype(BF16)
        split[s, 0] = high
        split[s, 1] = (whole - high.astype(F32)).astype(BF16)

    weights = []
    for s in range(2):
        row_block = r * 8 + rows_ref[s]
        half = cols_ref[s] // 8
        col_block = (c + COLS * half) * 8 + (cols_ref[s] - 8 * half)
        live = jnp.where(row_block == col_block, 0.5, 1.0)
        weights.append(jnp.where(s < count_ref[0], live, 0.0).astype(F32))

    pl.semaphore_wait(barrier, 15 + 31 + 64)

    def send_vectors(k):
        src = sent.at[k]
        slot = COLS * (r // COLS) + c

        def to_twin(n):
            target = lax.rem(r + n, ROWS)
            push(src, vcol.at[k, slot], v_send.at[k], vcol_sem.at[k, r // COLS], at(target, twin))

        loop(1, ROWS, to_twin)

        @pl.when(own)
        def _():
            vcol[k, slot] = sent[k]

        @pl.when(jnp.logical_not(own))
        def _():
            to_twin(0)

        def to_col(n):
            push(src, vrow.at[k, c], v_send.at[k], vrow_sem.at[k], at(r, lax.rem(c + n, COLS)))

        loop(1, COLS, to_col)
        vrow[k, c] = sent[k]

    def drain_sized(ref, k, full, cond, sem):
        @pl.when(cond)
        def _():
            drain(ref.at[k, pl.ds(0, full - 1)], sem)

        @pl.when(jnp.logical_not(cond))
        def _():
            drain(ref.at[k, pl.ds(0, full)], sem)

    def products(k, inverse):
        drain(vrow.at[k, pl.ds(0, COLS - 1)], vrow_sem.at[k])
        terms = []
        for s in range(2):
            b = 2 * rows_ref[s]
            vec = jnp.concatenate([vrow[k, b], vrow[k, b + 1]], axis=1)
            term = dot(vec, split[s, 0], None) + dot(vec, split[s, 1], None)
            terms.append(term if inverse is None else dot(inverse, term))
        for b in range(2 * 8):
            part = sum(terms[s] * jnp.where(cols_ref[s] == b, weights[s], 0.0) for s in range(2)).astype(BF16)
            pcol[k, 2 * b] = part[:, :LANES]
            pcol[k, 2 * b + 1] = part[:, LANES:]

        def to_col_owner(n):
            n16 = lax.rem(c + n, COLS)
            for h in range(2):
                push(pcol.at[k, COLS * h + n16], gcol.at[k, r], p_send.at[k], gcol_sem.at[k], at(c + COLS * h, n16))

        loop(1, COLS, to_col_owner)
        for h in range(2):
            mine = r == c + COLS * h

            @pl.when(mine)
            def _():
                gcol[k, r] = pcol[k, COLS * h + c]

            @pl.when(jnp.logical_not(mine))
            def _():
                push(pcol.at[k, COLS * h + c], gcol.at[k, r], p_send.at[k], gcol_sem.at[k], at(c + COLS * h, c))

        for h in range(2):

            @pl.when(r == c + COLS * h)
            def _():
                drain(vcol.at[k, pl.ds(0, COLS - 1)], vcol_sem.at[k, h])

            @pl.when(r != c + COLS * h)
            def _():
                drain(vcol.at[k, pl.ds(0, COLS)], vcol_sem.at[k, h])

        terms = []
        for s in range(2):
            b = 2 * cols_ref[s]
            vec = jnp.concatenate([vcol[k, b], vcol[k, b + 1]], axis=1)
            term = dot_t(vec, split[s, 0], None) + dot_t(vec, split[s, 1], None)
            terms.append(term if inverse is None else dot(inverse, term))
        for b in range(8):
            part = sum(terms[s] * jnp.where(rows_ref[s] == b, weights[s], 0.0) for s in range(2)).astype(BF16)
            prow[k, 2 * b] = part[:, :LANES]
            prow[k, 2 * b + 1] = part[:, LANES:]

        def to_row_owner(n):
            n16 = lax.rem(c + n, COLS)
            push(prow.at[k, n16], grow.at[k, c], p_send.at[k], grow_sem.at[k], at(r, n16))

        loop(1, COLS, to_row_owner)
        grow[k, c] = prow[k, c]

    def image(k, current):
        drain_sized(gcol, k, ROWS, own, gcol_sem.at[k])
        drain(grow.at[k, pl.ds(0, COLS - 1)], grow_sem.at[k])
        total = dg[...] * current
        total += jnp.sum(gcol[k].astype(F32), axis=0)
        total += jnp.sum(grow[k].astype(F32), axis=0)
        return total

    def inner_send(k, w):
        stack[IMAGE : IMAGE + BW, :] = w
        partial = dot_t(w, stack[...])
        for n in range(BW):
            c_part[k, n] = partial[n : n + 1, :]

        def to_col(n):
            n16 = lax.rem(c + n, COLS)
            push(c_part.at[k, n16], c_col.at[k, c], ar_send.at[k, 0], ar_sem.at[k, 0], at(r, n16))

        loop(1, COLS, to_col)
        c_col[k, c] = c_part[k, c]

    def inner_rows(k):
        drain(c_col.at[k, pl.ds(0, COLS - 1)], ar_sem.at[k, 0])
        c_sum[k] = jnp.sum(c_col[k], axis=0)

        def to_row(n):
            push(c_sum.at[k], c_row.at[k, r], ar_send.at[k, 1], ar_sem.at[k, 1], at(lax.rem(r + n, ROWS), c))

        loop(1, ROWS, to_row)
        c_row[k, r] = c_sum[k]

    def inner_cols(k):
        drain(c_row.at[k, pl.ds(0, ROWS - 1)], ar_sem.at[k, 1])
        c_all[k] = jnp.sum(c_row[k], axis=0) * inv_total

        def to_col(n):
            push(c_all.at[k], c_got.at[k, c], ar_send.at[k, 2], ar_sem.at[k, 2], at(r, lax.rem(c + n, COLS)))

        loop(1, COLS, to_col)
        c_got[k, c] = c_all[k]

    def inner_done(k):
        drain(c_got.at[k, pl.ds(0, COLS - 1)], ar_sem.at[k, 2])
        total = jnp.concatenate([c_got[k, n] for n in range(BW)], axis=0)
        lane = lax.broadcasted_iota(jnp.int32, (BW, DEPTH), 1)
        return jnp.where(lane < IMAGE, total, 0.0), total[:, IMAGE : IMAGE + BW]

    def gram_of(first, square):
        both = 2.0 * first - dot(first, gram[...])
        rest = first - dot(both, gram[...])
        return square - dot_t(first, both) - dot_t(both, rest), rest

    def gram_cols():
        def to_col(n):
            n16 = lax.rem(c + n, COLS)
            push(m_part.at[n16], m_col.at[c], m_send.at[0], m_sem.at[0], at(r, n16))

        loop(1, COLS, to_col)

    def gram_y():
        drain(m_col.at[pl.ds(0, COLS - 1)], m_sem.at[0])
        m_one[...] = jnp.sum(m_col[...], axis=0)

        def to_y(n):
            push(m_one, m_y.at[y], m_send.at[1], m_sem.at[1], at(lax.rem(y + n, YS) * XS + x, c))

        loop(1, YS, to_y)
        m_y[y] = m_one[...]

    def gram_x():
        drain(m_y.at[pl.ds(0, YS - 1)], m_sem.at[1])
        m_two[...] = jnp.sum(m_y[...], axis=0)

        def to_x(n):
            push(m_two, m_x.at[x], m_send.at[2], m_sem.at[2], at(y * XS + lax.rem(x + n, XS), c))

        loop(1, XS, to_x)
        m_x[x] = m_two[...]

    def gram_spread():
        drain(m_x.at[pl.ds(0, XS - 1)], m_sem.at[2])
        m_all[...] = jnp.sum(m_x[...], axis=0) * inv_total

        def to_col(n):
            push(m_all, m_got.at[c], m_send.at[3], m_sem.at[3], at(r, lax.rem(c + n, COLS)))

        loop(1, COLS, to_col)
        m_got[c] = m_all[...]

    def gram_build():
        drain(m_got.at[pl.ds(0, COLS - 1)], m_sem.at[3])
        top = m_got[:, 0].reshape(128, 128)
        side = m_got[:, 1].reshape(128, 128)
        under = m_got[:, 2].reshape(128, 128)
        gram[0:128, 0:128] = top
        gram[0:128, 128:256] = side
        gram[128:256, 0:128] = side.T
        gram[128:256, 128:256] = under
        gram[256:DEPTH, :] = jnp.zeros((128, DEPTH), F32)
        for n in range(COLS):
            for j in range(3):
                gram[256 + n : 257 + n, LANES * j : LANES * (j + 1)] = m_got[n, 3, j : j + 1, :]
        gram[0:128, 256:DEPTH] = gram[256:DEPTH, 0:128].T
        gram[128:256, 256:DEPTH] = gram[256:DEPTH, 128:256].T
        clean[...] = 2.0 * stack[...] - dot(gram[...], stack[...])

    def gram_grow(inverse, rest, fresh):
        border = dot(inverse, rest)
        lane = lax.broadcasted_iota(jnp.int32, (BW, LANES), 1)
        row = lax.broadcasted_iota(jnp.int32, (BW, LANES), 0)
        gram[FRESH : FRESH + BW, 0:256] = border[:, 0:256]
        corner = jnp.where(lane < BW, border[:, 256:DEPTH], 0.0)
        block = jnp.concatenate([jnp.zeros((BW, LANES), F32), corner, jnp.zeros((96, LANES), F32)], axis=0)
        gram[256:DEPTH, 256:DEPTH] = gram[256:DEPTH, 256:DEPTH] + block + block.T
        gram[FRESH : FRESH + BW, 256:DEPTH] = corner + (lane == row + BW).astype(F32)
        gram[0:128, 256:DEPTH] = gram[256:DEPTH, 0:128].T
        gram[128:256, 256:DEPTH] = gram[256:DEPTH, 128:256].T
        clean[...] = 2.0 * stack[...] - dot(gram[...], stack[...])

    send_vectors(0)
    gram_cols()
    products(0, None)
    gram_y()
    w = image(0, last)
    inner_send(0, w)
    gram_x()
    inner_rows(0)
    gram_spread()
    inner_cols(0)
    gram_build()
    first, square = inner_done(0)
    w2 = w - dot(first, clean[...])
    sent[1] = w2.astype(BF16)
    send_vectors(1)
    square, rest = gram_of(first, square)
    lower, inverse = factor(square)
    factors_ref[0] = lower
    x1 = dot(inverse, w2)
    blocks_ref[0] = x1
    products(1, inverse)
    stack[FRESH : FRESH + BW, :] = x1
    gram_grow(inverse, rest, x1)
    w = image(1, x1)
    inner_send(1, w)
    inner_rows(1)
    inner_cols(1)
    first, square = inner_done(1)
    w2 = w - dot(first, clean[...])
    square, _ = gram_of(first, square)
    lower, inverse = factor(square)
    factors_ref[1] = lower
    blocks_ref[1] = dot(inverse, w2)

    for k in range(2):

        @pl.when(own)
        def _():
            drain(vcol.at[k, pl.ds(0, 31)], v_send.at[k])
            drain(gcol.at[k, pl.ds(0, 31)], p_send.at[k])

        @pl.when(jnp.logical_not(own))
        def _():
            drain(vcol.at[k, pl.ds(0, 32)], v_send.at[k])
            drain(gcol.at[k, pl.ds(0, 32)], p_send.at[k])

        drain(vrow.at[k, pl.ds(0, 15)], v_send.at[k])
        drain(grow.at[k, pl.ds(0, 15)], p_send.at[k])
        drain(c_col.at[k, pl.ds(0, 15)], ar_send.at[k, 0])
        drain(c_row.at[k, pl.ds(0, 31)], ar_send.at[k, 1])
        drain(c_got.at[k, pl.ds(0, 15)], ar_send.at[k, 2])
    drain(m_col.at[pl.ds(0, 15)], m_send.at[0])
    drain(m_y.at[pl.ds(0, 7)], m_send.at[1])
    drain(m_x.at[pl.ds(0, 3)], m_send.at[2])
    drain(m_got.at[pl.ds(0, 15)], m_send.at[3])


def local(tiles, tile_rows, tile_cols, tile_counts, diagonal, basis, start):
    any_spec = pl.BlockSpec(memory_space=pl.ANY)
    smem = pl.BlockSpec(memory_space=pltpu.SMEM)
    vmem = pl.BlockSpec(memory_space=pltpu.VMEM)
    dma = pltpu.SemaphoreType.DMA
    return pl.pallas_call(
        kernel,
        out_shape=(
            jax.ShapeDtypeStruct((2, BW, LANES), F32),
            jax.ShapeDtypeStruct((2, BW, BW), F32),
        ),
        in_specs=[any_spec, smem, smem, smem, any_spec, any_spec, any_spec],
        out_specs=(vmem, vmem),
        scratch_shapes=[
            pltpu.VMEM((DEPTH, LANES), F32),
            pltpu.VMEM((2, TILE, TILE), F32),
            pltpu.VMEM((2, 2, TILE, TILE), BF16),
            pltpu.VMEM((1, LANES), F32),
            pltpu.VMEM((2, BW, LANES), BF16),
            pltpu.VMEM((2, COLS, BW, LANES), BF16),
            pltpu.VMEM((2, 2 * COLS, BW, LANES), BF16),
            pltpu.VMEM((2, COLS, BW, LANES), BF16),
            pltpu.VMEM((2, 2 * COLS, BW, LANES), BF16),
            pltpu.VMEM((2, COLS, BW, LANES), BF16),
            pltpu.VMEM((2, ROWS, BW, LANES), BF16),
            pltpu.VMEM((2, COLS, 1, DEPTH), F32),
            pltpu.VMEM((2, COLS, 1, DEPTH), F32),
            pltpu.VMEM((2, 1, DEPTH), F32),
            pltpu.VMEM((2, ROWS, 1, DEPTH), F32),
            pltpu.VMEM((2, 1, DEPTH), F32),
            pltpu.VMEM((2, COLS, 1, DEPTH), F32),
            pltpu.VMEM((COLS, 4, 8, LANES), F32),
            pltpu.VMEM((COLS, 4, 8, LANES), F32),
            pltpu.VMEM((YS, 4, 8, LANES), F32),
            pltpu.VMEM((XS, 4, 8, LANES), F32),
            pltpu.VMEM((4, 8, LANES), F32),
            pltpu.VMEM((4, 8, LANES), F32),
            pltpu.VMEM((4, 8, LANES), F32),
            pltpu.VMEM((COLS, 4, 8, LANES), F32),
            pltpu.VMEM((DEPTH, DEPTH), F32),
            pltpu.VMEM((DEPTH, LANES), F32),
            dma((4,)),
            dma((2,)),
            dma((2,)),
            dma((2, 2)),
            dma((2,)),
            dma((2,)),
            dma((2,)),
            dma((2, 3)),
            dma((2, 3)),
            dma((4,)),
            dma((4,)),
        ],
        compiler_params=pltpu.CompilerParams(
            collective_id=0, has_side_effects=True, vmem_limit_bytes=48 * 1024 * 1024
        ),
    )(
        tiles.reshape(2, TILE, TILE),
        tile_rows.reshape(2),
        tile_cols.reshape(2),
        tile_counts.reshape(1),
        diagonal.reshape(1, LANES),
        basis.reshape(256, LANES),
        start,
    )


def solution(mesh):
    placed = (
        P("row", "col", None, None, None),
        P("row", "col", None),
        P("row", "col", None),
        P("row", "col"),
        P(("row", "col")),
        P(None, None, ("row", "col")),
        P(None, ("row", "col")),
    )
    return jax.shard_map(
        local,
        mesh=mesh,
        in_specs=placed,
        out_specs=(P(None, None, ("row", "col")), P()),
        check_vma=False,
    )
```

```python
import functools

import jax
import jax.numpy as jnp
from jax import lax
from jax.experimental import pallas as pl
from jax.experimental.pallas import tpu as pltpu
from jax.sharding import PartitionSpec as P

MESH = pl.DeviceIdType.MESH
F32, BF16 = jnp.float32, jnp.bfloat16
HIGH = lax.Precision.HIGHEST
ROWS, COLS, YS, XS = 32, 16, 8, 4
BW, LANES, TILE = 16, 128, 256
KNOWN, FRESH, IMAGE, DEPTH = 272, 272, 288, 384


def dot(a, b, precision=HIGH):
    return lax.dot_general(a, b, (((1,), (0,)), ((), ())), precision=precision, preferred_element_type=F32)


def dot_t(a, b, precision=HIGH):
    return lax.dot_general(a, b, (((1,), (1,)), ((), ())), precision=precision, preferred_element_type=F32)


def at(row, col):
    return {"row": row, "col": col}


def push(src, dst, send_sem, recv_sem, target):
    pltpu.make_async_remote_copy(
        src_ref=src, dst_ref=dst, send_sem=send_sem, recv_sem=recv_sem, device_id=target, device_id_type=MESH
    ).start()


def drain(ref, sem):
    pltpu.make_async_copy(ref, ref, sem).wait()


def loop(low, high, body):
    def run(k, carry):
        body(k)
        return carry

    lax.fori_loop(low, high, run, 0)


def far(n, size):
    return size // 2 + (2 * lax.rem(n, 2) - 1) * lax.div(n + 1, 2)


def factor(gram):
    row = lax.broadcasted_iota(jnp.int32, (BW, LANES), 0)
    lane = lax.broadcasted_iota(jnp.int32, (BW, LANES), 1)
    eye = (lane == row + BW).astype(F32)
    work = jnp.concatenate([gram, jnp.zeros((BW, LANES - BW), F32)], axis=1) + eye
    lower = jnp.zeros((BW, LANES), F32)
    scale = jnp.zeros((BW, LANES), F32)
    for j in range(BW):
        pivot_row = work[j : j + 1, :]
        column = work[:, j : j + 1]
        pivot = pivot_row[:, j : j + 1]
        root = 1.0 / jnp.sqrt(pivot)
        lower = jnp.where((lane == j) & (row >= j), column * root, lower)
        scale = jnp.where(row == j, root, scale)
        step = jnp.where(row > j, column * (1.0 / pivot), 0.0)
        work = work - step * pivot_row
    inverse = (work * scale)[:, BW : 2 * BW]
    return lower[:, :BW], inverse


def kernel(
    tiles_ref, rows_ref, cols_ref, count_ref, diag_ref, basis_ref, start_ref,
    blocks_ref, factors_ref,
    stack, plates, split, dg, sent, vrow, vcol, prow, pcol, grow, gcol,
    c_part, c_col, c_sum, c_row, c_all, c_got,
    m_part, m_twin, m_half, m_col, m_y, m_x, m_one, m_two, m_all, m_got, gram, clean, fold,
    load_sem, v_send, vrow_sem, vcol_sem, p_send, grow_sem, gcol_sem, ar_send, ar_sem, m_send, m_sem,
):
    r, c = lax.axis_index("row"), lax.axis_index("col")
    y, x = r // XS, lax.rem(r, XS)
    z, core = c // 2, lax.rem(c, 2)
    twin = lax.rem(r, COLS)
    own = c == twin
    inv_total = 1.0 / (ROWS * COLS * LANES)

    def row_at(n):
        return lax.rem(y + far(lax.div(n, XS), YS), YS) * XS + lax.rem(x + far(lax.rem(n, XS), XS), XS)

    def col_at(n):
        return lax.rem(c + far(n, COLS), COLS)

    loads = [
        pltpu.make_async_copy(basis_ref, stack.at[pl.ds(0, 256)], load_sem.at[0]),
        pltpu.make_async_copy(start_ref, stack.at[pl.ds(256, BW)], load_sem.at[1]),
        pltpu.make_async_copy(tiles_ref.at[0, 0], plates, load_sem.at[2]),
        pltpu.make_async_copy(diag_ref, dg, load_sem.at[3]),
    ]
    for each in loads:
        each.start()

    barrier = pltpu.get_barrier_semaphore()

    def greet(target):
        pl.semaphore_signal(barrier, inc=1, device_id=target, device_id_type=MESH)

    def greet_rows(k):
        greet(at(lax.rem(r + k, ROWS), c))

    def greet_cols(k):
        greet(at(r, lax.rem(c + k, COLS)))

    def greet_twins(k):
        greet(at(lax.rem(r + k, ROWS), twin))
        greet(at(c + COLS * (k // COLS), lax.rem(k, COLS)))

    loop(0, ROWS, greet_twins)
    loop(1, ROWS, greet_rows)
    loop(1, COLS, greet_cols)

    stack[FRESH:DEPTH, :] = jnp.zeros((DEPTH - FRESH, LANES), F32)
    loads[0].wait()
    loads[1].wait()
    low, mid, last = stack[0:128, :], stack[128:256, :], stack[256:DEPTH, :][:BW]
    sent[0] = last.astype(BF16)
    m_part[:, :, 0] = dot_t(low, low).reshape(2, 8, 8, LANES)
    m_part[:, :, 1] = dot_t(low, mid).reshape(2, 8, 8, LANES)
    m_part[:, :, 2] = dot_t(mid, mid).reshape(2, 8, 8, LANES)
    edge = dot_t(last, stack[...])
    m_part[:, :, 3] = jnp.zeros((2, 8, 8, LANES), F32)
    for k in range(COLS):
        for j in range(3):
            m_part[k // 8, k % 8, 3, j : j + 1, :] = edge[k : k + 1, LANES * j : LANES * (j + 1)]
    loads[2].wait()
    loads[3].wait()
    for s in range(2):
        whole = plates[s]
        high = whole.astype(BF16)
        split[s, 0] = high
        split[s, 1] = (whole - high.astype(F32)).astype(BF16)

    weights = []
    for s in range(2):
        row_block = r * 8 + rows_ref[0, 0, s]
        half = cols_ref[0, 0, s] // 8
        col_block = (c + COLS * half) * 8 + (cols_ref[0, 0, s] - 8 * half)
        live = jnp.where(row_block == col_block, 0.5, 1.0)
        weights.append(jnp.where(s < count_ref[0, 0], live, 0.0).astype(F32))

    pl.semaphore_wait(barrier, 15 + 31 + 64)

    def send_vectors(k):
        src = sent.at[k]
        slot = COLS * (r // COLS) + c

        def to_twin(n):
            target = row_at(n)
            push(src, vcol.at[k, slot], v_send.at[k], vcol_sem.at[k, r // COLS], at(target, twin))

        loop(0, ROWS - 1, to_twin)

        @pl.when(own)
        def _():
            vcol[k, slot] = sent[k]

        @pl.when(jnp.logical_not(own))
        def _():
            to_twin(ROWS - 1)

        def to_col(n):
            push(src, vrow.at[k, c], v_send.at[k], vrow_sem.at[k], at(r, col_at(n)))

        loop(0, COLS - 1, to_col)
        vrow[k, c] = sent[k]

    def drain_sized(ref, k, full, cond, sem):
        @pl.when(cond)
        def _():
            drain(ref.at[k, pl.ds(0, full - 1)], sem)

        @pl.when(jnp.logical_not(cond))
        def _():
            drain(ref.at[k, pl.ds(0, full)], sem)

    def products(k):
        drain(vrow.at[k, pl.ds(0, COLS - 1)], vrow_sem.at[k])
        terms = []
        for s in range(2):
            b = 2 * rows_ref[0, 0, s]
            vec = jnp.concatenate([vrow[k, b], vrow[k, b + 1]], axis=1)
            term = dot(vec, split[s, 0], None) + dot(vec, split[s, 1], None)
            terms.append(term)
        for b in range(2 * 8):
            part = sum(terms[s] * jnp.where(cols_ref[0, 0, s] == b, weights[s], 0.0) for s in range(2)).astype(BF16)
            pcol[k, 2 * (b % 8), b // 8] = part[:, :LANES]
            pcol[k, 2 * (b % 8) + 1, b // 8] = part[:, LANES:]

        def to_col_owner(n):
            target = col_at(n)
            for h in range(2):

                @pl.when(jnp.logical_or(target != c, r != c + COLS * h))
                def _():
                    push(pcol.at[k, target, h], gcol.at[k, r], p_send.at[k], gcol_sem.at[k], at(c + COLS * h, target))

        loop(0, COLS, to_col_owner)
        for h in range(2):

            @pl.when(r == c + COLS * h)
            def _():
                gcol[k, r] = pcol[k, c, h]

        for h in range(2):

            @pl.when(r == c + COLS * h)
            def _():
                drain(vcol.at[k, pl.ds(0, COLS - 1)], vcol_sem.at[k, h])

            @pl.when(r != c + COLS * h)
            def _():
                drain(vcol.at[k, pl.ds(0, COLS)], vcol_sem.at[k, h])

        terms = []
        for s in range(2):
            b = 2 * cols_ref[0, 0, s]
            vec = jnp.concatenate([vcol[k, b], vcol[k, b + 1]], axis=1)
            term = dot_t(vec, split[s, 0], None) + dot_t(vec, split[s, 1], None)
            terms.append(term)
        for b in range(8):
            part = sum(terms[s] * jnp.where(rows_ref[0, 0, s] == b, weights[s], 0.0) for s in range(2)).astype(BF16)
            prow[k, 2 * b] = part[:, :LANES]
            prow[k, 2 * b + 1] = part[:, LANES:]

        def to_row_owner(n):
            n16 = col_at(n)
            push(prow.at[k, n16], grow.at[k, c], p_send.at[k], grow_sem.at[k], at(r, n16))

        loop(0, COLS - 1, to_row_owner)
        grow[k, c] = prow[k, c]

    def image(k, current):
        drain_sized(gcol, k, ROWS, own, gcol_sem.at[k])
        drain(grow.at[k, pl.ds(0, COLS - 1)], grow_sem.at[k])
        total = dg[...] * current
        total += jnp.sum(gcol[k].astype(F32), axis=0)
        total += jnp.sum(grow[k].astype(F32), axis=0)
        return total

    def inner_send(k, w):
        stack[IMAGE : IMAGE + BW, :] = w
        partial = dot_t(w, stack[...])
        for n in range(BW):
            c_part[k, n] = partial[n : n + 1, :]

        def to_col(n):
            n16 = col_at(n)
            push(c_part.at[k, n16], c_col.at[k, c], ar_send.at[k, 0], ar_sem.at[k, 0], at(r, n16))

        loop(0, COLS - 1, to_col)
        c_col[k, c] = c_part[k, c]

    def inner_rows(k):
        drain(c_col.at[k, pl.ds(0, COLS - 1)], ar_sem.at[k, 0])
        c_sum[k] = jnp.sum(c_col[k], axis=0)

        def to_row(n):
            push(c_sum.at[k], c_row.at[k, r], ar_send.at[k, 1], ar_sem.at[k, 1], at(row_at(n), c))

        loop(0, ROWS - 1, to_row)
        c_row[k, r] = c_sum[k]

    def inner_cols(k):
        drain(c_row.at[k, pl.ds(0, ROWS - 1)], ar_sem.at[k, 1])
        c_all[k] = jnp.sum(c_row[k], axis=0) * inv_total

        def to_col(n):
            push(c_all.at[k], c_got.at[k, c], ar_send.at[k, 2], ar_sem.at[k, 2], at(r, col_at(n)))

        loop(0, COLS - 1, to_col)
        c_got[k, c] = c_all[k]

    def inner_done(k):
        drain(c_got.at[k, pl.ds(0, COLS - 1)], ar_sem.at[k, 2])
        total = jnp.concatenate([c_got[k, n] for n in range(BW)], axis=0)
        lane = lax.broadcasted_iota(jnp.int32, (BW, DEPTH), 1)
        return jnp.where(lane < IMAGE, total, 0.0), total[:, IMAGE : IMAGE + BW]

    def gram_of(first, square):
        both = 2.0 * first - dot(first, gram[...])
        rest = first - dot(both, gram[...])
        return square - dot_t(first, both) - dot_t(both, rest), rest

    def gram_pair():
        push(m_part.at[1 - core], m_twin, m_send.at[4], m_sem.at[4], at(r, c + 1 - 2 * core))

    def gram_z():
        drain(m_twin, m_sem.at[4])
        m_half[...] = m_part[core] + m_twin[...]

        def to_z(n):
            target = lax.rem(z + far(n, YS), YS)
            push(m_half.at[target], m_col.at[z], m_send.at[0], m_sem.at[0], at(r, 2 * target + core))

        loop(0, YS - 1, to_z)
        m_col[z] = m_half[z]

    def gram_y():
        drain(m_col.at[pl.ds(0, YS - 1)], m_sem.at[0])
        m_one[...] = jnp.sum(m_col[...], axis=0)

        def to_y(n):
            push(m_one, m_y.at[y], m_send.at[1], m_sem.at[1], at(lax.rem(y + n, YS) * XS + x, c))

        loop(1, YS, to_y)
        m_y[y] = m_one[...]

    def gram_x():
        drain(m_y.at[pl.ds(0, YS - 1)], m_sem.at[1])
        m_two[...] = jnp.sum(m_y[...], axis=0)

        def to_x(n):
            push(m_two, m_x.at[x], m_send.at[2], m_sem.at[2], at(y * XS + lax.rem(x + n, XS), c))

        loop(1, XS, to_x)
        m_x[x] = m_two[...]

    def gram_spread():
        drain(m_x.at[pl.ds(0, XS - 1)], m_sem.at[2])
        m_all[...] = jnp.sum(m_x[...], axis=0) * inv_total

        def to_z(n):
            target = lax.rem(z + far(n, YS), YS)
            push(m_all, m_got.at[core, z], m_send.at[3], m_sem.at[3], at(r, 2 * target + core))

        loop(0, YS - 1, to_z)
        m_got[core, z] = m_all[...]

    def gram_share():
        drain(m_col.at[pl.ds(0, YS - 1)], m_sem.at[3])
        push(m_got.at[core], m_got.at[core], m_send.at[5], m_sem.at[5], at(r, c + 1 - 2 * core))

    def gram_build():
        drain(m_twin, m_sem.at[5])
        top = m_got[:, :, 0].reshape(128, 128)
        side = m_got[:, :, 1].reshape(128, 128)
        under = m_got[:, :, 2].reshape(128, 128)
        gram[0:128, 0:128] = top
        gram[0:128, 128:256] = side
        gram[128:256, 0:128] = side.T
        gram[128:256, 128:256] = under
        gram[256:DEPTH, :] = jnp.zeros((128, DEPTH), F32)
        for n in range(COLS):
            for j in range(3):
                gram[256 + n : 257 + n, LANES * j : LANES * (j + 1)] = m_got[n // 8, n % 8, 3, j : j + 1, :]
        gram[0:128, 256:DEPTH] = gram[256:DEPTH, 0:128].T
        gram[128:256, 256:DEPTH] = gram[256:DEPTH, 128:256].T
        clean[...] = 2.0 * stack[...] - dot(gram[...], stack[...])

    def gram_grow(inverse, rest, fresh):
        border = dot(inverse, rest)
        lane = lax.broadcasted_iota(jnp.int32, (BW, LANES), 1)
        row = lax.broadcasted_iota(jnp.int32, (BW, LANES), 0)
        gram[FRESH : FRESH + BW, 0:256] = border[:, 0:256]
        corner = jnp.where(lane < BW, border[:, 256:DEPTH], 0.0)
        block = jnp.concatenate([jnp.zeros((BW, LANES), F32), corner, jnp.zeros((96, LANES), F32)], axis=0)
        gram[256:DEPTH, 256:DEPTH] = gram[256:DEPTH, 256:DEPTH] + block + block.T
        gram[FRESH : FRESH + BW, 256:DEPTH] = corner + (lane == row + BW).astype(F32)
        gram[0:128, 256:DEPTH] = gram[256:DEPTH, 0:128].T
        gram[128:256, 256:DEPTH] = gram[256:DEPTH, 128:256].T
        clean[...] = 2.0 * stack[...] - dot(gram[...], stack[...])

    def gram_fold():
        row = lax.broadcasted_iota(jnp.int32, (DEPTH, DEPTH), 0)
        lane = lax.broadcasted_iota(jnp.int32, (DEPTH, DEPTH), 1)
        eye = (row == lane).astype(F32)
        off = eye - gram[...]
        fold[...] = eye + off
        fold[...] += dot(fold[...], dot(off, off))

    gram_pair()
    send_vectors(0)
    gram_z()
    products(0)
    gram_y()
    w = image(0, last)
    inner_send(0, w)
    gram_x()
    inner_rows(0)
    gram_spread()
    inner_cols(0)
    gram_share()
    gram_build()
    first, square = inner_done(0)
    w2 = w - dot(first, clean[...])
    sent[1] = w2.astype(BF16)
    send_vectors(1)
    square, rest = gram_of(first, square)
    lower, inverse = factor(square)
    factors_ref[0] = lower
    x1 = dot(inverse, w2)
    blocks_ref[0] = x1
    products(1)
    stack[FRESH : FRESH + BW, :] = x1
    gram_grow(inverse, rest, x1)
    gram_fold()
    w = dot(inverse, image(1, w2))
    inner_send(1, w)
    inner_rows(1)
    inner_cols(1)
    first, square = inner_done(1)
    w2 = w - dot(first, clean[...])
    square -= dot_t(first, dot(first, fold[...]))
    lower, inverse = factor(square)
    factors_ref[1] = lower
    blocks_ref[1] = dot(inverse, w2)

    for k in range(2):

        @pl.when(own)
        def _():
            drain(vcol.at[k, pl.ds(0, 31)], v_send.at[k])
            drain(gcol.at[k, pl.ds(0, 31)], p_send.at[k])

        @pl.when(jnp.logical_not(own))
        def _():
            drain(vcol.at[k, pl.ds(0, 32)], v_send.at[k])
            drain(gcol.at[k, pl.ds(0, 32)], p_send.at[k])

        drain(vrow.at[k, pl.ds(0, 15)], v_send.at[k])
        drain(grow.at[k, pl.ds(0, 15)], p_send.at[k])
        drain(c_col.at[k, pl.ds(0, 15)], ar_send.at[k, 0])
        drain(c_row.at[k, pl.ds(0, 31)], ar_send.at[k, 1])
        drain(c_got.at[k, pl.ds(0, 15)], ar_send.at[k, 2])
    drain(m_col.at[pl.ds(0, 7)], m_send.at[0])
    drain(m_y.at[pl.ds(0, 7)], m_send.at[1])
    drain(m_x.at[pl.ds(0, 3)], m_send.at[2])
    drain(m_col.at[pl.ds(0, 7)], m_send.at[3])
    drain(m_twin, m_send.at[4])
    drain(m_twin, m_send.at[5])


def local(tiles, tile_rows, tile_cols, tile_counts, diagonal, basis, start):
    any_spec = pl.BlockSpec(memory_space=pltpu.HBM)
    smem = pl.BlockSpec(memory_space=pltpu.SMEM)
    vmem = pl.BlockSpec(memory_space=pltpu.VMEM)
    dma = pltpu.SemaphoreType.DMA
    return pl.pallas_call(
        kernel,
        out_shape=(
            jax.ShapeDtypeStruct((2, BW, LANES), F32),
            jax.ShapeDtypeStruct((2, BW, BW), F32),
        ),
        in_specs=[any_spec, smem, smem, smem, any_spec, any_spec, any_spec],
        out_specs=(vmem, vmem),
        scratch_shapes=[
            pltpu.VMEM((DEPTH, LANES), F32),
            pltpu.VMEM((2, TILE, TILE), F32),
            pltpu.VMEM((2, 2, TILE, TILE), BF16),
            pltpu.VMEM((1, LANES), F32),
            pltpu.VMEM((2, BW, LANES), BF16),
            pltpu.VMEM((2, COLS, BW, LANES), BF16),
            pltpu.VMEM((2, 2 * COLS, BW, LANES), BF16),
            pltpu.VMEM((2, COLS, BW, LANES), BF16),
            pltpu.VMEM((2, COLS, 2, BW, LANES), BF16),
            pltpu.VMEM((2, COLS, BW, LANES), BF16),
            pltpu.VMEM((2, ROWS, BW, LANES), BF16),
            pltpu.VMEM((2, COLS, 1, DEPTH), F32),
            pltpu.VMEM((2, COLS, 1, DEPTH), F32),
            pltpu.VMEM((2, 1, DEPTH), F32),
            pltpu.VMEM((2, ROWS, 1, DEPTH), F32),
            pltpu.VMEM((2, 1, DEPTH), F32),
            pltpu.VMEM((2, COLS, 1, DEPTH), F32),
            pltpu.VMEM((2, 8, 4, 8, LANES), F32),
            pltpu.VMEM((8, 4, 8, LANES), F32),
            pltpu.VMEM((8, 4, 8, LANES), F32),
            pltpu.VMEM((8, 4, 8, LANES), F32),
            pltpu.VMEM((YS, 4, 8, LANES), F32),
            pltpu.VMEM((XS, 4, 8, LANES), F32),
            pltpu.VMEM((4, 8, LANES), F32),
            pltpu.VMEM((4, 8, LANES), F32),
            pltpu.VMEM((4, 8, LANES), F32),
            pltpu.VMEM((2, 8, 4, 8, LANES), F32),
            pltpu.VMEM((DEPTH, DEPTH), F32),
            pltpu.VMEM((DEPTH, LANES), F32),
            pltpu.VMEM((DEPTH, DEPTH), F32),
            dma((4,)),
            dma((2,)),
            dma((2,)),
            dma((2, 2)),
            dma((2,)),
            dma((2,)),
            dma((2,)),
            dma((2, 3)),
            dma((2, 3)),
            dma((6,)),
            dma((6,)),
        ],
        compiler_params=pltpu.CompilerParams(
            collective_id=0, has_side_effects=True, vmem_limit_bytes=60 * 1024 * 1024
        ),
    )(
        tiles,
        tile_rows,
        tile_cols,
        tile_counts,
        diagonal.reshape(1, LANES),
        basis.reshape(256, LANES),
        start,
    )


def solution(mesh):
    placed = (
        P("row", "col", None, None, None),
        P("row", "col", None),
        P("row", "col", None),
        P("row", "col"),
        P(("row", "col")),
        P(None, None, ("row", "col")),
        P(None, ("row", "col")),
    )
    return jax.shard_map(
        local,
        mesh=mesh,
        in_specs=placed,
        out_specs=(P(None, None, ("row", "col")), P()),
        check_vma=False,
    )
```

```python
import functools

import jax
import jax.numpy as jnp
from jax import lax
from jax.experimental import pallas as pl
from jax.experimental.pallas import tpu as pltpu
from jax.sharding import PartitionSpec as P

MESH = pl.DeviceIdType.MESH
F32, BF16 = jnp.float32, jnp.bfloat16
HIGH = lax.Precision.HIGHEST
ROWS, COLS, YS, XS = 32, 16, 8, 4
BW, LANES, TILE = 16, 128, 256
KNOWN, FRESH, IMAGE, DEPTH = 272, 272, 288, 384


def dot(a, b, precision=HIGH):
    return lax.dot_general(a, b, (((1,), (0,)), ((), ())), precision=precision, preferred_element_type=F32)


def dot_t(a, b, precision=HIGH):
    return lax.dot_general(a, b, (((1,), (1,)), ((), ())), precision=precision, preferred_element_type=F32)


def at(row, col):
    return {"row": row, "col": col}


def push(src, dst, send_sem, recv_sem, target):
    pltpu.make_async_remote_copy(
        src_ref=src, dst_ref=dst, send_sem=send_sem, recv_sem=recv_sem, device_id=target, device_id_type=MESH
    ).start()


def drain(ref, sem):
    pltpu.make_async_copy(ref, ref, sem).wait()


def loop(low, high, body):
    def run(k, carry):
        body(k)
        return carry

    lax.fori_loop(low, high, run, 0)


def far(n, size):
    return size // 2 + (2 * lax.rem(n, 2) - 1) * lax.div(n + 1, 2)


def factor(gram):
    row = lax.broadcasted_iota(jnp.int32, (BW, LANES), 0)
    lane = lax.broadcasted_iota(jnp.int32, (BW, LANES), 1)
    eye = (lane == row + BW).astype(F32)
    work = jnp.concatenate([gram, jnp.zeros((BW, LANES - BW), F32)], axis=1) + eye
    lower = jnp.zeros((BW, LANES), F32)
    scale = jnp.zeros((BW, LANES), F32)
    for j in range(BW):
        pivot_row = work[j : j + 1, :]
        column = work[:, j : j + 1]
        pivot = pivot_row[:, j : j + 1]
        root = 1.0 / jnp.sqrt(pivot)
        lower = jnp.where((lane == j) & (row >= j), column * root, lower)
        scale = jnp.where(row == j, root, scale)
        step = jnp.where(row > j, column * (1.0 / pivot), 0.0)
        work = work - step * pivot_row
    inverse = (work * scale)[:, BW : 2 * BW]
    return lower[:, :BW], inverse


def kernel(
    tiles_ref, rows_ref, cols_ref, count_ref, diag_ref, basis_ref, start_ref,
    blocks_ref, factors_ref,
    stack, plates, split, dg, sent, vrow, vcol, prow, pcol, grow, gcol,
    c_part, c_col, c_sum, c_row, c_all, c_got,
    m_part, m_twin, m_half, m_x, m_one, m_y, m_two, m_z, m_all, m_back, m_got, gram, clean, fold,
    load_sem, v_send, vrow_sem, vcol_sem, p_send, grow_sem, gcol_sem, ar_send, ar_sem, m_send, m_sem,
):
    r, c = lax.axis_index("row"), lax.axis_index("col")
    y, x = r // XS, lax.rem(r, XS)
    z, core = c // 2, lax.rem(c, 2)
    twin = lax.rem(r, COLS)
    own = c == twin
    inv_total = 1.0 / (ROWS * COLS * LANES)

    def row_at(n):
        return lax.rem(y + far(lax.div(n, XS), YS), YS) * XS + lax.rem(x + far(lax.rem(n, XS), XS), XS)

    def col_at(n):
        return lax.rem(c + far(n, COLS), COLS)

    loads = [
        pltpu.make_async_copy(basis_ref, stack.at[pl.ds(0, 256)], load_sem.at[0]),
        pltpu.make_async_copy(start_ref, stack.at[pl.ds(256, BW)], load_sem.at[1]),
        pltpu.make_async_copy(tiles_ref.at[0, 0], plates, load_sem.at[2]),
        pltpu.make_async_copy(diag_ref, dg, load_sem.at[3]),
    ]
    for each in loads:
        each.start()

    barrier = pltpu.get_barrier_semaphore()

    def greet(target):
        pl.semaphore_signal(barrier, inc=1, device_id=target, device_id_type=MESH)

    def greet_rows(k):
        greet(at(row_at(k), c))

    def greet_cols(k):
        greet(at(r, col_at(k)))

    def greet_twins(k):
        greet(at(row_at(k), twin))
        greet(at(c + COLS * lax.rem(k, 2), col_at(lax.div(k, 2))))

    loop(0, ROWS, greet_twins)
    loop(0, ROWS - 1, greet_rows)
    loop(0, COLS - 1, greet_cols)

    stack[FRESH:DEPTH, :] = jnp.zeros((DEPTH - FRESH, LANES), F32)
    loads[0].wait()
    loads[1].wait()
    low, mid, last = stack[0:128, :], stack[128:256, :], stack[256:DEPTH, :][:BW]
    sent[0] = last.astype(BF16)
    m_part[:, :, :, 0] = dot_t(low, low).reshape(2, 4, 2, 8, LANES)
    m_part[:, :, :, 1] = dot_t(low, mid).reshape(2, 4, 2, 8, LANES)
    m_part[:, :, :, 2] = dot_t(mid, mid).reshape(2, 4, 2, 8, LANES)
    edge = dot_t(last, stack[...])
    m_part[:, :, :, 3] = jnp.zeros((2, 4, 2, 8, LANES), F32)
    for k in range(COLS):
        for j in range(3):
            m_part[k // 8, k % 8 // 2, k % 2, 3, j : j + 1, :] = edge[k : k + 1, LANES * j : LANES * (j + 1)]
    loads[2].wait()
    loads[3].wait()
    for s in range(2):
        whole = plates[s]
        high = whole.astype(BF16)
        split[s, 0] = high
        split[s, 1] = (whole - high.astype(F32)).astype(BF16)

    weights = []
    for s in range(2):
        row_block = r * 8 + rows_ref[0, 0, s]
        half = cols_ref[0, 0, s] // 8
        col_block = (c + COLS * half) * 8 + (cols_ref[0, 0, s] - 8 * half)
        live = jnp.where(row_block == col_block, 0.5, 1.0)
        weights.append(jnp.where(s < count_ref[0, 0], live, 0.0).astype(F32))

    pl.semaphore_wait(barrier, 15 + 31 + 64)

    def send_vectors(k):
        src = sent.at[k]
        slot = COLS * (r // COLS) + c

        def to_twin(n):
            target = row_at(n)
            push(src, vcol.at[k, slot], v_send.at[k], vcol_sem.at[k, r // COLS], at(target, twin))

        loop(0, ROWS - 1, to_twin)

        @pl.when(own)
        def _():
            vcol[k, slot] = sent[k]

        @pl.when(jnp.logical_not(own))
        def _():
            to_twin(ROWS - 1)

        def to_col(n):
            push(src, vrow.at[k, c], v_send.at[k], vrow_sem.at[k], at(r, col_at(n)))

        loop(0, COLS - 1, to_col)
        vrow[k, c] = sent[k]

    def drain_sized(ref, k, full, cond, sem):
        @pl.when(cond)
        def _():
            drain(ref.at[k, pl.ds(0, full - 1)], sem)

        @pl.when(jnp.logical_not(cond))
        def _():
            drain(ref.at[k, pl.ds(0, full)], sem)

    def products(k):
        drain(vrow.at[k, pl.ds(0, COLS - 1)], vrow_sem.at[k])
        terms = []
        for s in range(2):
            b = 2 * rows_ref[0, 0, s]
            vec = jnp.concatenate([vrow[k, b], vrow[k, b + 1]], axis=1)
            term = dot(vec, split[s, 0], None) + dot(vec, split[s, 1], None)
            terms.append(term)
        for b in range(2 * 8):
            part = sum(terms[s] * jnp.where(cols_ref[0, 0, s] == b, weights[s], 0.0) for s in range(2)).astype(BF16)
            pcol[k, 2 * (b % 8), b // 8] = part[:, :LANES]
            pcol[k, 2 * (b % 8) + 1, b // 8] = part[:, LANES:]

        def to_col_owner(n):
            target = col_at(n)
            for h in range(2):

                @pl.when(jnp.logical_or(target != c, r != c + COLS * h))
                def _():
                    push(pcol.at[k, target, h], gcol.at[k, r], p_send.at[k], gcol_sem.at[k], at(c + COLS * h, target))

        loop(0, COLS, to_col_owner)
        for h in range(2):

            @pl.when(r == c + COLS * h)
            def _():
                gcol[k, r] = pcol[k, c, h]

        for h in range(2):

            @pl.when(r == c + COLS * h)
            def _():
                drain(vcol.at[k, pl.ds(0, COLS - 1)], vcol_sem.at[k, h])

            @pl.when(r != c + COLS * h)
            def _():
                drain(vcol.at[k, pl.ds(0, COLS)], vcol_sem.at[k, h])

        terms = []
        for s in range(2):
            b = 2 * cols_ref[0, 0, s]
            vec = jnp.concatenate([vcol[k, b], vcol[k, b + 1]], axis=1)
            term = dot_t(vec, split[s, 0], None) + dot_t(vec, split[s, 1], None)
            terms.append(term)
        for b in range(8):
            part = sum(terms[s] * jnp.where(rows_ref[0, 0, s] == b, weights[s], 0.0) for s in range(2)).astype(BF16)
            prow[k, 2 * b] = part[:, :LANES]
            prow[k, 2 * b + 1] = part[:, LANES:]

        def to_row_owner(n):
            n16 = col_at(n)
            push(prow.at[k, n16], grow.at[k, c], p_send.at[k], grow_sem.at[k], at(r, n16))

        loop(0, COLS - 1, to_row_owner)
        grow[k, c] = prow[k, c]

    def image(k, current):
        drain_sized(gcol, k, ROWS, own, gcol_sem.at[k])
        drain(grow.at[k, pl.ds(0, COLS - 1)], grow_sem.at[k])
        total = dg[...] * current
        total += jnp.sum(gcol[k].astype(F32), axis=0)
        total += jnp.sum(grow[k].astype(F32), axis=0)
        return total

    def inner_send(k, w):
        stack[IMAGE : IMAGE + BW, :] = w
        partial = dot_t(w, stack[...])
        for n in range(BW):
            c_part[k, n] = partial[n : n + 1, :]

        def to_col(n):
            n16 = col_at(n)
            push(c_part.at[k, n16], c_col.at[k, c], ar_send.at[k, 0], ar_sem.at[k, 0], at(r, n16))

        loop(0, COLS - 1, to_col)
        c_col[k, c] = c_part[k, c]

    def inner_rows(k):
        drain(c_col.at[k, pl.ds(0, COLS - 1)], ar_sem.at[k, 0])
        c_sum[k] = jnp.sum(c_col[k], axis=0)

        def to_row(n):
            push(c_sum.at[k], c_row.at[k, r], ar_send.at[k, 1], ar_sem.at[k, 1], at(row_at(n), c))

        loop(0, ROWS - 1, to_row)
        c_row[k, r] = c_sum[k]

    def inner_cols(k):
        drain(c_row.at[k, pl.ds(0, ROWS - 1)], ar_sem.at[k, 1])
        c_all[k] = jnp.sum(c_row[k], axis=0) * inv_total

        def to_col(n):
            push(c_all.at[k], c_got.at[k, c], ar_send.at[k, 2], ar_sem.at[k, 2], at(r, col_at(n)))

        loop(0, COLS - 1, to_col)
        c_got[k, c] = c_all[k]

    def inner_done(k):
        drain(c_got.at[k, pl.ds(0, COLS - 1)], ar_sem.at[k, 2])
        total = jnp.concatenate([c_got[k, n] for n in range(BW)], axis=0)
        lane = lax.broadcasted_iota(jnp.int32, (BW, DEPTH), 1)
        return jnp.where(lane < IMAGE, total, 0.0), total[:, IMAGE : IMAGE + BW]

    def gram_of(first, square):
        both = 2.0 * first - dot(first, gram[...])
        rest = first - dot(both, gram[...])
        return square - dot_t(first, both) - dot_t(both, rest), rest

    def gram_pair():
        push(m_part.at[1 - core], m_twin, m_send.at[4], m_sem.at[4], at(r, c + 1 - 2 * core))

    def gram_x():
        drain(m_twin, m_sem.at[4])
        m_half[...] = m_part[core] + m_twin[...]

        def to_x(n):
            target = lax.rem(x + far(n, XS), XS)
            push(m_half.at[target], m_x.at[x], m_send.at[0], m_sem.at[0], at(y * XS + target, c))

        loop(0, XS - 1, to_x)
        m_x[x] = m_half[x]

    def gram_y():
        drain(m_x.at[pl.ds(0, XS - 1)], m_sem.at[0])
        m_one[...] = jnp.sum(m_x[...], axis=0)

        def to_y(n):
            target = lax.rem(y + far(n, YS), YS)
            piece = m_one.at[lax.div(target, 4), lax.rem(target, 4)]
            push(piece, m_y.at[y], m_send.at[1], m_sem.at[1], at(target * XS + x, c))

        loop(0, YS - 1, to_y)
        m_y[y] = m_one[lax.div(y, 4), lax.rem(y, 4)]

    def gram_z():
        drain(m_y.at[pl.ds(0, YS - 1)], m_sem.at[1])
        m_two[...] = jnp.sum(m_y[...], axis=0)

        def to_z(n):
            target = lax.rem(z + far(n, 8), 8)
            push(m_two, m_z.at[z], m_send.at[2], m_sem.at[2], at(r, 2 * target + core))

        loop(0, 7, to_z)
        m_z[z] = m_two[...]

    def gram_y_back():
        drain(m_z.at[pl.ds(0, 7)], m_sem.at[2])
        m_all[...] = jnp.sum(m_z[...], axis=0) * inv_total
        mine = lax.div(y, 4), lax.rem(y, 4)

        def to_y(n):
            target = lax.rem(y + far(n, YS), YS)
            push(m_all, m_back.at[mine], m_send.at[3], m_sem.at[3], at(target * XS + x, c))

        loop(0, YS - 1, to_y)
        m_back[mine] = m_all[...]

    def gram_x_back():
        drain(m_z.at[pl.ds(0, 7)], m_sem.at[3])

        def to_x(n):
            target = lax.rem(x + far(n, XS), XS)
            push(m_back, m_got.at[core, x], m_send.at[6], m_sem.at[6], at(y * XS + target, c))

        loop(0, XS - 1, to_x)
        m_got[core, x] = m_back[...]

    def gram_share():
        drain(m_x.at[pl.ds(0, XS - 1)], m_sem.at[6])
        push(m_got.at[core], m_got.at[core], m_send.at[5], m_sem.at[5], at(r, c + 1 - 2 * core))

    def gram_build():
        drain(m_twin, m_sem.at[5])
        top = m_got[:, :, :, 0].reshape(128, 128)
        side = m_got[:, :, :, 1].reshape(128, 128)
        under = m_got[:, :, :, 2].reshape(128, 128)
        gram[0:128, 0:128] = top
        gram[0:128, 128:256] = side
        gram[128:256, 0:128] = side.T
        gram[128:256, 128:256] = under
        gram[256:DEPTH, :] = jnp.zeros((128, DEPTH), F32)
        for n in range(COLS):
            for j in range(3):
                gram[256 + n : 257 + n, LANES * j : LANES * (j + 1)] = m_got[n // 8, n % 8 // 2, n % 2, 3, j : j + 1, :]
        gram[0:128, 256:DEPTH] = gram[256:DEPTH, 0:128].T
        gram[128:256, 256:DEPTH] = gram[256:DEPTH, 128:256].T
        clean[...] = 2.0 * stack[...] - dot(gram[...], stack[...])

    def gram_grow(inverse, rest, fresh):
        border = dot(inverse, rest)
        lane = lax.broadcasted_iota(jnp.int32, (BW, LANES), 1)
        row = lax.broadcasted_iota(jnp.int32, (BW, LANES), 0)
        gram[FRESH : FRESH + BW, 0:256] = border[:, 0:256]
        corner = jnp.where(lane < BW, border[:, 256:DEPTH], 0.0)
        block = jnp.concatenate([jnp.zeros((BW, LANES), F32), corner, jnp.zeros((96, LANES), F32)], axis=0)
        gram[256:DEPTH, 256:DEPTH] = gram[256:DEPTH, 256:DEPTH] + block + block.T
        gram[FRESH : FRESH + BW, 256:DEPTH] = corner + (lane == row + BW).astype(F32)
        gram[0:128, 256:DEPTH] = gram[256:DEPTH, 0:128].T
        gram[128:256, 256:DEPTH] = gram[256:DEPTH, 128:256].T
        clean[...] = 2.0 * stack[...] - dot(gram[...], stack[...])

    def gram_fold():
        row = lax.broadcasted_iota(jnp.int32, (DEPTH, DEPTH), 0)
        lane = lax.broadcasted_iota(jnp.int32, (DEPTH, DEPTH), 1)
        eye = (row == lane).astype(F32)
        off = eye - gram[...]
        fold[...] = eye + off
        fold[...] += dot(fold[...], dot(off, off))

    gram_pair()
    send_vectors(0)
    gram_x()
    products(0)
    gram_y()
    gram_z()
    w = image(0, last)
    inner_send(0, w)
    gram_y_back()
    inner_rows(0)
    gram_x_back()
    inner_cols(0)
    gram_share()
    gram_build()
    first, square = inner_done(0)
    w2 = w - dot(first, clean[...])
    sent[1] = w2.astype(BF16)
    send_vectors(1)
    square, rest = gram_of(first, square)
    lower, inverse = factor(square)
    factors_ref[0] = lower
    x1 = dot(inverse, w2)
    blocks_ref[0] = x1
    products(1)
    stack[FRESH : FRESH + BW, :] = x1
    gram_grow(inverse, rest, x1)
    gram_fold()
    w = dot(inverse, image(1, w2))
    inner_send(1, w)
    inner_rows(1)
    inner_cols(1)
    first, square = inner_done(1)
    w2 = w - dot(first, clean[...])
    square -= dot_t(first, dot(first, fold[...]))
    lower, inverse = factor(square)
    factors_ref[1] = lower
    blocks_ref[1] = dot(inverse, w2)

    for k in range(2):

        @pl.when(own)
        def _():
            drain(vcol.at[k, pl.ds(0, 31)], v_send.at[k])
            drain(gcol.at[k, pl.ds(0, 31)], p_send.at[k])

        @pl.when(jnp.logical_not(own))
        def _():
            drain(vcol.at[k, pl.ds(0, 32)], v_send.at[k])
            drain(gcol.at[k, pl.ds(0, 32)], p_send.at[k])

        drain(vrow.at[k, pl.ds(0, 15)], v_send.at[k])
        drain(grow.at[k, pl.ds(0, 15)], p_send.at[k])
        drain(c_col.at[k, pl.ds(0, 15)], ar_send.at[k, 0])
        drain(c_row.at[k, pl.ds(0, 31)], ar_send.at[k, 1])
        drain(c_got.at[k, pl.ds(0, 15)], ar_send.at[k, 2])
    drain(m_x.at[pl.ds(0, 3)], m_send.at[0])
    drain(m_y.at[pl.ds(0, 7)], m_send.at[1])
    drain(m_y.at[pl.ds(0, 7)], m_send.at[2])
    drain(m_y.at[pl.ds(0, 7)], m_send.at[3])
    drain(m_twin, m_send.at[4])
    drain(m_twin, m_send.at[5])
    drain(m_x.at[pl.ds(0, 3)], m_send.at[6])


def local(tiles, tile_rows, tile_cols, tile_counts, diagonal, basis, start):
    any_spec = pl.BlockSpec(memory_space=pltpu.HBM)
    smem = pl.BlockSpec(memory_space=pltpu.SMEM)
    vmem = pl.BlockSpec(memory_space=pltpu.VMEM)
    dma = pltpu.SemaphoreType.DMA
    return pl.pallas_call(
        kernel,
        out_shape=(
            jax.ShapeDtypeStruct((2, BW, LANES), F32),
            jax.ShapeDtypeStruct((2, BW, BW), F32),
        ),
        in_specs=[any_spec, smem, smem, smem, any_spec, any_spec, any_spec],
        out_specs=(vmem, vmem),
        scratch_shapes=[
            pltpu.VMEM((DEPTH, LANES), F32),
            pltpu.VMEM((2, TILE, TILE), F32),
            pltpu.VMEM((2, 2, TILE, TILE), BF16),
            pltpu.VMEM((1, LANES), F32),
            pltpu.VMEM((2, BW, LANES), BF16),
            pltpu.VMEM((2, COLS, BW, LANES), BF16),
            pltpu.VMEM((2, 2 * COLS, BW, LANES), BF16),
            pltpu.VMEM((2, COLS, BW, LANES), BF16),
            pltpu.VMEM((2, COLS, 2, BW, LANES), BF16),
            pltpu.VMEM((2, COLS, BW, LANES), BF16),
            pltpu.VMEM((2, ROWS, BW, LANES), BF16),
            pltpu.VMEM((2, COLS, 1, DEPTH), F32),
            pltpu.VMEM((2, COLS, 1, DEPTH), F32),
            pltpu.VMEM((2, 1, DEPTH), F32),
            pltpu.VMEM((2, ROWS, 1, DEPTH), F32),
            pltpu.VMEM((2, 1, DEPTH), F32),
            pltpu.VMEM((2, COLS, 1, DEPTH), F32),
            pltpu.VMEM((2, XS, 2, 4, 8, LANES), F32),
            pltpu.VMEM((XS, 2, 4, 8, LANES), F32),
            pltpu.VMEM((XS, 2, 4, 8, LANES), F32),
            pltpu.VMEM((XS, 2, 4, 8, LANES), F32),
            pltpu.VMEM((2, 4, 8, LANES), F32),
            pltpu.VMEM((YS, 8, LANES), F32),
            pltpu.VMEM((8, LANES), F32),
            pltpu.VMEM((8, 8, LANES), F32),
            pltpu.VMEM((8, LANES), F32),
            pltpu.VMEM((2, 4, 8, LANES), F32),
            pltpu.VMEM((2, XS, 2, 4, 8, LANES), F32),
            pltpu.VMEM((DEPTH, DEPTH), F32),
            pltpu.VMEM((DEPTH, LANES), F32),
            pltpu.VMEM((DEPTH, DEPTH), F32),
            dma((4,)),
            dma((2,)),
            dma((2,)),
            dma((2, 2)),
            dma((2,)),
            dma((2,)),
            dma((2,)),
            dma((2, 3)),
            dma((2, 3)),
            dma((7,)),
            dma((7,)),
        ],
        compiler_params=pltpu.CompilerParams(
            collective_id=0, has_side_effects=True, vmem_limit_bytes=60 * 1024 * 1024
        ),
    )(
        tiles,
        tile_rows,
        tile_cols,
        tile_counts,
        diagonal.reshape(1, LANES),
        basis.reshape(256, LANES),
        start,
    )


def solution(mesh):
    placed = (
        P("row", "col", None, None, None),
        P("row", "col", None),
        P("row", "col", None),
        P("row", "col"),
        P(("row", "col")),
        P(None, None, ("row", "col")),
        P(None, ("row", "col")),
    )
    return jax.shard_map(
        local,
        mesh=mesh,
        in_specs=placed,
        out_specs=(P(None, None, ("row", "col")), P()),
        check_vma=False,
    )
```

```python
import functools

import jax
import jax.numpy as jnp
from jax import lax
from jax.experimental import pallas as pl
from jax.experimental.pallas import tpu as pltpu
from jax.sharding import PartitionSpec as P

MESH = pl.DeviceIdType.MESH
F32, BF16 = jnp.float32, jnp.bfloat16
HIGH = lax.Precision.HIGHEST
ROWS, COLS, YS, XS = 32, 16, 8, 4
BW, LANES, TILE = 16, 128, 256
KNOWN, FRESH, IMAGE, DEPTH = 272, 272, 288, 384


def dot(a, b, precision=HIGH):
    return lax.dot_general(a, b, (((1,), (0,)), ((), ())), precision=precision, preferred_element_type=F32)


def dot_t(a, b, precision=HIGH):
    return lax.dot_general(a, b, (((1,), (1,)), ((), ())), precision=precision, preferred_element_type=F32)


def at(row, col):
    return {"row": row, "col": col}


def push(src, dst, send_sem, recv_sem, target):
    pltpu.make_async_remote_copy(
        src_ref=src, dst_ref=dst, send_sem=send_sem, recv_sem=recv_sem, device_id=target, device_id_type=MESH
    ).start()


def drain(ref, sem):
    pltpu.make_async_copy(ref, ref, sem).wait()


def loop(low, high, body):
    def run(k, carry):
        body(k)
        return carry

    lax.fori_loop(low, high, run, 0)


def far(n, size):
    return size // 2 + (2 * lax.rem(n, 2) - 1) * lax.div(n + 1, 2)


def factor(gram):
    row = lax.broadcasted_iota(jnp.int32, (BW, LANES), 0)
    lane = lax.broadcasted_iota(jnp.int32, (BW, LANES), 1)
    eye = (lane == row + BW).astype(F32)
    work = jnp.concatenate([gram, jnp.zeros((BW, LANES - BW), F32)], axis=1) + eye
    lower = jnp.zeros((BW, LANES), F32)
    scale = jnp.zeros((BW, LANES), F32)
    for j in range(0, BW, 2):
        row_one, row_two = work[j : j + 1, :], work[j + 1 : j + 2, :]
        col_one, col_two = work[:, j : j + 1], work[:, j + 1 : j + 2]
        one, side, two = row_one[:, j : j + 1], row_one[:, j + 1 : j + 2], row_two[:, j + 1 : j + 2]
        share = 1.0 / one
        ratio = side * share
        two = two - ratio * side
        root_one, root_two = 1.0 / jnp.sqrt(one), 1.0 / jnp.sqrt(two)
        row_two = row_two - ratio * row_one
        col_two = col_two - ratio * col_one
        lower = jnp.where((lane == j) & (row >= j), col_one * root_one, lower)
        lower = jnp.where((lane == j + 1) & (row > j), col_two * root_two, lower)
        scale = jnp.where(row == j, root_one, jnp.where(row == j + 1, root_two, scale))
        step = jnp.where(row > j + 1, col_one * (share * row_one) + col_two * ((1.0 / two) * row_two), 0.0)
        work = jnp.where(row == j + 1, row_two, work - step)
    inverse = (work * scale)[:, BW : 2 * BW]
    return lower[:, :BW], inverse


def kernel(
    tiles_ref, rows_ref, cols_ref, count_ref, diag_ref, basis_ref, start_ref,
    blocks_ref, factors_ref,
    stack, plates, split, dg, sent, vrow, vcol, prow, pcol, grow, gcol,
    c_part, c_col, c_sum, c_row, c_all, c_got,
    m_part, m_twin, m_half, m_x, m_one, m_y, m_two, m_z, m_all, m_back, m_got, gram, clean, fold,
    load_sem, v_send, vrow_sem, vcol_sem, p_send, grow_sem, gcol_sem, ar_send, ar_sem, m_send, m_sem,
):
    r, c = lax.axis_index("row"), lax.axis_index("col")
    y, x = r // XS, lax.rem(r, XS)
    z, core = c // 2, lax.rem(c, 2)
    twin = lax.rem(r, COLS)
    own = c == twin
    inv_total = 1.0 / (ROWS * COLS * LANES)

    def row_at(n):
        return lax.rem(y + far(lax.div(n, XS), YS), YS) * XS + lax.rem(x + far(lax.rem(n, XS), XS), XS)

    def col_at(n):
        return lax.rem(c + far(n, COLS), COLS)

    loads = [
        pltpu.make_async_copy(basis_ref, stack.at[pl.ds(0, 256)], load_sem.at[0]),
        pltpu.make_async_copy(start_ref, stack.at[pl.ds(256, BW)], load_sem.at[1]),
        pltpu.make_async_copy(tiles_ref.at[0, 0], plates, load_sem.at[2]),
        pltpu.make_async_copy(diag_ref, dg, load_sem.at[3]),
    ]
    for each in loads:
        each.start()

    barrier = pltpu.get_barrier_semaphore()

    def greet(target):
        pl.semaphore_signal(barrier, inc=1, device_id=target, device_id_type=MESH)

    def greet_rows(k):
        greet(at(row_at(k), c))

    def greet_cols(k):
        greet(at(r, col_at(k)))

    def greet_twins(k):
        greet(at(row_at(k), twin))
        greet(at(c + COLS * lax.rem(k, 2), col_at(lax.div(k, 2))))

    loop(0, ROWS, greet_twins)
    loop(0, ROWS - 1, greet_rows)
    loop(0, COLS - 1, greet_cols)

    stack[FRESH:DEPTH, :] = jnp.zeros((DEPTH - FRESH, LANES), F32)
    loads[0].wait()
    loads[1].wait()
    low, mid, last = stack[0:128, :], stack[128:256, :], stack[256:DEPTH, :][:BW]
    sent[0] = last.astype(BF16)
    m_part[:, :, :, 0] = dot_t(low, low).reshape(2, 4, 2, 8, LANES)
    m_part[:, :, :, 1] = dot_t(low, mid).reshape(2, 4, 2, 8, LANES)
    m_part[:, :, :, 2] = dot_t(mid, mid).reshape(2, 4, 2, 8, LANES)
    edge = dot_t(last, stack[...])
    m_part[:, :, :, 3] = jnp.zeros((2, 4, 2, 8, LANES), F32)
    for k in range(COLS):
        for j in range(3):
            m_part[k // 8, k % 8 // 2, k % 2, 3, j : j + 1, :] = edge[k : k + 1, LANES * j : LANES * (j + 1)]
    loads[2].wait()
    loads[3].wait()
    for s in range(2):
        whole = plates[s]
        high = whole.astype(BF16)
        split[s, 0] = high
        split[s, 1] = (whole - high.astype(F32)).astype(BF16)

    weights = []
    for s in range(2):
        row_block = r * 8 + rows_ref[0, 0, s]
        half = cols_ref[0, 0, s] // 8
        col_block = (c + COLS * half) * 8 + (cols_ref[0, 0, s] - 8 * half)
        live = jnp.where(row_block == col_block, 0.5, 1.0)
        weights.append(jnp.where(s < count_ref[0, 0], live, 0.0).astype(F32))

    pl.semaphore_wait(barrier, 15 + 31 + 64)

    def send_vectors(k):
        src = sent.at[k]
        slot = COLS * (r // COLS) + c

        def to_twin(n):
            target = row_at(n)
            push(src, vcol.at[k, slot], v_send.at[k], vcol_sem.at[k, r // COLS], at(target, twin))

        def to_col(n):
            push(src, vrow.at[k, c], v_send.at[k], vrow_sem.at[k], at(r, col_at(n)))

        loop(0, COLS - 1, to_col)
        loop(0, ROWS - 1, to_twin)

        @pl.when(own)
        def _():
            vcol[k, slot] = sent[k]

        @pl.when(jnp.logical_not(own))
        def _():
            to_twin(ROWS - 1)

        vrow[k, c] = sent[k]

    def drain_sized(ref, k, full, cond, sem):
        @pl.when(cond)
        def _():
            drain(ref.at[k, pl.ds(0, full - 1)], sem)

        @pl.when(jnp.logical_not(cond))
        def _():
            drain(ref.at[k, pl.ds(0, full)], sem)

    def products(k):
        drain(vrow.at[k, pl.ds(0, COLS - 1)], vrow_sem.at[k])
        terms = []
        for s in range(2):
            b = 2 * rows_ref[0, 0, s]
            vec = jnp.concatenate([vrow[k, b], vrow[k, b + 1]], axis=1)
            term = dot(vec, split[s, 0], None) + dot(vec, split[s, 1], None)
            terms.append(term)
        for b in range(2 * 8):
            part = sum(terms[s] * jnp.where(cols_ref[0, 0, s] == b, weights[s], 0.0) for s in range(2)).astype(BF16)
            pcol[k, 2 * (b % 8), b // 8] = part[:, :LANES]
            pcol[k, 2 * (b % 8) + 1, b // 8] = part[:, LANES:]

        def to_col_owner(n):
            target = col_at(n)
            for h in range(2):

                @pl.when(jnp.logical_or(target != c, r != c + COLS * h))
                def _():
                    push(pcol.at[k, target, h], gcol.at[k, r], p_send.at[k], gcol_sem.at[k], at(c + COLS * h, target))

        loop(0, COLS, to_col_owner)
        for h in range(2):

            @pl.when(r == c + COLS * h)
            def _():
                gcol[k, r] = pcol[k, c, h]

        for h in range(2):

            @pl.when(r == c + COLS * h)
            def _():
                drain(vcol.at[k, pl.ds(0, COLS - 1)], vcol_sem.at[k, h])

            @pl.when(r != c + COLS * h)
            def _():
                drain(vcol.at[k, pl.ds(0, COLS)], vcol_sem.at[k, h])

        terms = []
        for s in range(2):
            b = 2 * cols_ref[0, 0, s]
            vec = jnp.concatenate([vcol[k, b], vcol[k, b + 1]], axis=1)
            term = dot_t(vec, split[s, 0], None) + dot_t(vec, split[s, 1], None)
            terms.append(term)
        for b in range(8):
            part = sum(terms[s] * jnp.where(rows_ref[0, 0, s] == b, weights[s], 0.0) for s in range(2)).astype(BF16)
            prow[k, 2 * b] = part[:, :LANES]
            prow[k, 2 * b + 1] = part[:, LANES:]

        def to_row_owner(n):
            n16 = col_at(n)
            push(prow.at[k, n16], grow.at[k, c], p_send.at[k], grow_sem.at[k], at(r, n16))

        loop(0, COLS - 1, to_row_owner)
        grow[k, c] = prow[k, c]

    def image(k, current):
        drain_sized(gcol, k, ROWS, own, gcol_sem.at[k])
        drain(grow.at[k, pl.ds(0, COLS - 1)], grow_sem.at[k])
        total = dg[...] * current
        total += jnp.sum(gcol[k].astype(F32), axis=0)
        total += jnp.sum(grow[k].astype(F32), axis=0)
        return total

    def inner_send(k, w):
        stack[IMAGE : IMAGE + BW, :] = w
        partial = dot_t(w, stack[...])
        for n in range(BW):
            c_part[k, n] = partial[n : n + 1, :]

        def to_col(n):
            n16 = col_at(n)
            push(c_part.at[k, n16], c_col.at[k, c], ar_send.at[k, 0], ar_sem.at[k, 0], at(r, n16))

        loop(0, COLS - 1, to_col)
        c_col[k, c] = c_part[k, c]

    def inner_rows(k):
        drain(c_col.at[k, pl.ds(0, COLS - 1)], ar_sem.at[k, 0])
        c_sum[k] = jnp.sum(c_col[k], axis=0)

        def to_row(n):
            push(c_sum.at[k], c_row.at[k, r], ar_send.at[k, 1], ar_sem.at[k, 1], at(row_at(n), c))

        loop(0, ROWS - 1, to_row)
        c_row[k, r] = c_sum[k]

    def inner_cols(k):
        drain(c_row.at[k, pl.ds(0, ROWS - 1)], ar_sem.at[k, 1])
        c_all[k] = jnp.sum(c_row[k], axis=0) * inv_total

        def to_col(n):
            push(c_all.at[k], c_got.at[k, c], ar_send.at[k, 2], ar_sem.at[k, 2], at(r, col_at(n)))

        loop(0, COLS - 1, to_col)
        c_got[k, c] = c_all[k]

    def inner_done(k):
        drain(c_got.at[k, pl.ds(0, COLS - 1)], ar_sem.at[k, 2])
        total = jnp.concatenate([c_got[k, n] for n in range(BW)], axis=0)
        lane = lax.broadcasted_iota(jnp.int32, (BW, DEPTH), 1)
        return jnp.where(lane < IMAGE, total, 0.0), total[:, IMAGE : IMAGE + BW]

    def gram_of(first, square):
        both = 2.0 * first - dot(first, gram[...])
        rest = first - dot(both, gram[...])
        return square - dot_t(first, both) - dot_t(both, rest), rest

    def gram_pair():
        push(m_part.at[1 - core], m_twin, m_send.at[4], m_sem.at[4], at(r, c + 1 - 2 * core))

    def gram_x():
        drain(m_twin, m_sem.at[4])
        m_half[...] = m_part[core] + m_twin[...]

        def to_x(n):
            target = lax.rem(x + far(n, XS), XS)
            push(m_half.at[target], m_x.at[x], m_send.at[0], m_sem.at[0], at(y * XS + target, c))

        loop(0, XS - 1, to_x)
        m_x[x] = m_half[x]

    def gram_y():
        drain(m_x.at[pl.ds(0, XS - 1)], m_sem.at[0])
        m_one[...] = jnp.sum(m_x[...], axis=0)

        def to_y(n):
            target = lax.rem(y + far(n, YS), YS)
            piece = m_one.at[lax.div(target, 4), lax.rem(target, 4)]
            push(piece, m_y.at[y], m_send.at[1], m_sem.at[1], at(target * XS + x, c))

        loop(0, YS - 1, to_y)
        m_y[y] = m_one[lax.div(y, 4), lax.rem(y, 4)]

    def gram_z():
        drain(m_y.at[pl.ds(0, YS - 1)], m_sem.at[1])
        m_two[...] = jnp.sum(m_y[...], axis=0)

        def to_z(n):
            target = lax.rem(z + far(n, 8), 8)
            push(m_two, m_z.at[z], m_send.at[2], m_sem.at[2], at(r, 2 * target + core))

        loop(0, 7, to_z)
        m_z[z] = m_two[...]

    def gram_y_back():
        drain(m_z.at[pl.ds(0, 7)], m_sem.at[2])
        m_all[...] = jnp.sum(m_z[...], axis=0) * inv_total
        mine = lax.div(y, 4), lax.rem(y, 4)

        def to_y(n):
            target = lax.rem(y + far(n, YS), YS)
            push(m_all, m_back.at[mine], m_send.at[3], m_sem.at[3], at(target * XS + x, c))

        loop(0, YS - 1, to_y)
        m_back[mine] = m_all[...]

    def gram_x_back():
        drain(m_z.at[pl.ds(0, 7)], m_sem.at[3])

        def to_x(n):
            target = lax.rem(x + far(n, XS), XS)
            push(m_back, m_got.at[core, x], m_send.at[6], m_sem.at[6], at(y * XS + target, c))

        loop(0, XS - 1, to_x)
        m_got[core, x] = m_back[...]

    def gram_share():
        drain(m_x.at[pl.ds(0, XS - 1)], m_sem.at[6])
        push(m_got.at[core], m_got.at[core], m_send.at[5], m_sem.at[5], at(r, c + 1 - 2 * core))

    def gram_build():
        drain(m_twin, m_sem.at[5])
        top = m_got[:, :, :, 0].reshape(128, 128)
        side = m_got[:, :, :, 1].reshape(128, 128)
        under = m_got[:, :, :, 2].reshape(128, 128)
        gram[0:128, 0:128] = top
        gram[0:128, 128:256] = side
        gram[128:256, 0:128] = side.T
        gram[128:256, 128:256] = under
        gram[256:DEPTH, :] = jnp.zeros((128, DEPTH), F32)
        for n in range(COLS):
            for j in range(3):
                gram[256 + n : 257 + n, LANES * j : LANES * (j + 1)] = m_got[n // 8, n % 8 // 2, n % 2, 3, j : j + 1, :]
        gram[0:128, 256:DEPTH] = gram[256:DEPTH, 0:128].T
        gram[128:256, 256:DEPTH] = gram[256:DEPTH, 128:256].T
        clean[...] = 2.0 * stack[...] - dot(gram[...], stack[...])

    def gram_grow(inverse, rest, fresh):
        border = dot(inverse, rest)
        lane = lax.broadcasted_iota(jnp.int32, (BW, LANES), 1)
        row = lax.broadcasted_iota(jnp.int32, (BW, LANES), 0)
        gram[FRESH : FRESH + BW, 0:256] = border[:, 0:256]
        corner = jnp.where(lane < BW, border[:, 256:DEPTH], 0.0)
        block = jnp.concatenate([jnp.zeros((BW, LANES), F32), corner, jnp.zeros((96, LANES), F32)], axis=0)
        gram[256:DEPTH, 256:DEPTH] = gram[256:DEPTH, 256:DEPTH] + block + block.T
        gram[FRESH : FRESH + BW, 256:DEPTH] = corner + (lane == row + BW).astype(F32)
        gram[0:128, 256:DEPTH] = gram[256:DEPTH, 0:128].T
        gram[128:256, 256:DEPTH] = gram[256:DEPTH, 128:256].T
        clean[...] = 2.0 * stack[...] - dot(gram[...], stack[...])

    def gram_fold():
        row = lax.broadcasted_iota(jnp.int32, (DEPTH, DEPTH), 0)
        lane = lax.broadcasted_iota(jnp.int32, (DEPTH, DEPTH), 1)
        eye = (row == lane).astype(F32)
        off = eye - gram[...]
        fold[...] = eye + off
        fold[...] += dot(fold[...], dot(off, off))

    gram_pair()
    send_vectors(0)
    gram_x()
    products(0)
    gram_y()
    gram_z()
    w = image(0, last)
    inner_send(0, w)
    gram_y_back()
    inner_rows(0)
    gram_x_back()
    inner_cols(0)
    gram_share()
    gram_build()
    first, square = inner_done(0)
    w2 = w - dot(first, clean[...])
    sent[1] = w2.astype(BF16)
    send_vectors(1)
    square, rest = gram_of(first, square)
    lower, inverse = factor(square)
    factors_ref[0] = lower
    x1 = dot(inverse, w2)
    blocks_ref[0] = x1
    products(1)
    stack[FRESH : FRESH + BW, :] = x1
    gram_grow(inverse, rest, x1)
    gram_fold()
    w = dot(inverse, image(1, w2))
    inner_send(1, w)
    inner_rows(1)
    inner_cols(1)
    first, square = inner_done(1)
    w2 = w - dot(first, clean[...])
    square -= dot_t(first, dot(first, fold[...]))
    lower, inverse = factor(square)
    factors_ref[1] = lower
    blocks_ref[1] = dot(inverse, w2)

    for k in range(2):

        @pl.when(own)
        def _():
            drain(vcol.at[k, pl.ds(0, 31)], v_send.at[k])
            drain(gcol.at[k, pl.ds(0, 31)], p_send.at[k])

        @pl.when(jnp.logical_not(own))
        def _():
            drain(vcol.at[k, pl.ds(0, 32)], v_send.at[k])
            drain(gcol.at[k, pl.ds(0, 32)], p_send.at[k])

        drain(vrow.at[k, pl.ds(0, 15)], v_send.at[k])
        drain(grow.at[k, pl.ds(0, 15)], p_send.at[k])
        drain(c_col.at[k, pl.ds(0, 15)], ar_send.at[k, 0])
        drain(c_row.at[k, pl.ds(0, 31)], ar_send.at[k, 1])
        drain(c_got.at[k, pl.ds(0, 15)], ar_send.at[k, 2])
    drain(m_x.at[pl.ds(0, 3)], m_send.at[0])
    drain(m_y.at[pl.ds(0, 7)], m_send.at[1])
    drain(m_y.at[pl.ds(0, 7)], m_send.at[2])
    drain(m_y.at[pl.ds(0, 7)], m_send.at[3])
    drain(m_twin, m_send.at[4])
    drain(m_twin, m_send.at[5])
    drain(m_x.at[pl.ds(0, 3)], m_send.at[6])


def local(tiles, tile_rows, tile_cols, tile_counts, diagonal, basis, start):
    any_spec = pl.BlockSpec(memory_space=pltpu.HBM)
    smem = pl.BlockSpec(memory_space=pltpu.SMEM)
    vmem = pl.BlockSpec(memory_space=pltpu.VMEM)
    dma = pltpu.SemaphoreType.DMA
    return pl.pallas_call(
        kernel,
        out_shape=(
            jax.ShapeDtypeStruct((2, BW, LANES), F32),
            jax.ShapeDtypeStruct((2, BW, BW), F32),
        ),
        in_specs=[any_spec, smem, smem, smem, any_spec, any_spec, any_spec],
        out_specs=(vmem, vmem),
        scratch_shapes=[
            pltpu.VMEM((DEPTH, LANES), F32),
            pltpu.VMEM((2, TILE, TILE), F32),
            pltpu.VMEM((2, 2, TILE, TILE), BF16),
            pltpu.VMEM((1, LANES), F32),
            pltpu.VMEM((2, BW, LANES), BF16),
            pltpu.VMEM((2, COLS, BW, LANES), BF16),
            pltpu.VMEM((2, 2 * COLS, BW, LANES), BF16),
            pltpu.VMEM((2, COLS, BW, LANES), BF16),
            pltpu.VMEM((2, COLS, 2, BW, LANES), BF16),
            pltpu.VMEM((2, COLS, BW, LANES), BF16),
            pltpu.VMEM((2, ROWS, BW, LANES), BF16),
            pltpu.VMEM((2, COLS, 1, DEPTH), F32),
            pltpu.VMEM((2, COLS, 1, DEPTH), F32),
            pltpu.VMEM((2, 1, DEPTH), F32),
            pltpu.VMEM((2, ROWS, 1, DEPTH), F32),
            pltpu.VMEM((2, 1, DEPTH), F32),
            pltpu.VMEM((2, COLS, 1, DEPTH), F32),
            pltpu.VMEM((2, XS, 2, 4, 8, LANES), F32),
            pltpu.VMEM((XS, 2, 4, 8, LANES), F32),
            pltpu.VMEM((XS, 2, 4, 8, LANES), F32),
            pltpu.VMEM((XS, 2, 4, 8, LANES), F32),
            pltpu.VMEM((2, 4, 8, LANES), F32),
            pltpu.VMEM((YS, 8, LANES), F32),
            pltpu.VMEM((8, LANES), F32),
            pltpu.VMEM((8, 8, LANES), F32),
            pltpu.VMEM((8, LANES), F32),
            pltpu.VMEM((2, 4, 8, LANES), F32),
            pltpu.VMEM((2, XS, 2, 4, 8, LANES), F32),
            pltpu.VMEM((DEPTH, DEPTH), F32),
            pltpu.VMEM((DEPTH, LANES), F32),
            pltpu.VMEM((DEPTH, DEPTH), F32),
            dma((4,)),
            dma((2,)),
            dma((2,)),
            dma((2, 2)),
            dma((2,)),
            dma((2,)),
            dma((2,)),
            dma((2, 3)),
            dma((2, 3)),
            dma((7,)),
            dma((7,)),
        ],
        compiler_params=pltpu.CompilerParams(
            collective_id=0, has_side_effects=True, vmem_limit_bytes=60 * 1024 * 1024
        ),
    )(
        tiles,
        tile_rows,
        tile_cols,
        tile_counts,
        diagonal.reshape(1, LANES),
        basis.reshape(256, LANES),
        start,
    )


def solution(mesh):
    placed = (
        P("row", "col", None, None, None),
        P("row", "col", None),
        P("row", "col", None),
        P("row", "col"),
        P(("row", "col")),
        P(None, None, ("row", "col")),
        P(None, ("row", "col")),
    )
    return jax.shard_map(
        local,
        mesh=mesh,
        in_specs=placed,
        out_specs=(P(None, None, ("row", "col")), P()),
        check_vma=False,
    )
```
